32 devices in a mesh: dp: 4 (over y, core), seq: 8 (over z, x).
Axes of the slice: x: 2, y: 2, z: 4, core: 2. Of those that a mesh axis runs over, the one named last changes fastest.
Arguments:
- queries: bfloat16 [8, 512, 4096], P('dp', 'seq'), may hold values from -140 to 140
- keys: bfloat16 [8, 512, 4096], P('dp', 'seq'), may hold values from -5.5 to 5.5
- values: bfloat16 [8, 512, 4096], P('dp', 'seq'), may hold values from -6 to 6
- teacher: bfloat16 [8, 640, 1536], P('dp', 'seq'), may hold values from -6 to 6
- resample_index: int32 [8, 512, 4], P('dp', 'seq'), may hold values from 0 to 639, as said below
- resample_frac: int32 [8, 512, 2], P('dp', 'seq'), may hold values from 0 to 7
- timesteps: int32 [8], P('dp'), may hold values from 0 to 999
- norm_gain: float32 [4096], replicated, may hold values from 0.1 to 1.9
- proj_in: bfloat16 [4096, 1024], P(('dp', 'seq')), may hold values from -0.09375 to 0.09375
- bias_in: float32 [1024], replicated, may hold values from -3 to 3
- proj_out: bfloat16 [1024, 1536], P(('dp', 'seq')), may hold values from -0.1875 to 0.1875
- bias_out: float32 [1536], replicated, may hold values from -3 to 3
Outputs:
- alignment: float32 [8, 512], P('dp', 'seq')
- grad_attended: bfloat16 [8, 512, 4096], P('dp', 'seq')
The draws below stay inside these ranges and needn't reach their ends.
Inputs may be any that keep to these rules, and one draw needn't show every extreme that they name: `resample_index`: every index of student token s lies in teacher rows (s // 64) * 80 - 8 to (s // 64 + 1) * 80 + 7.
All inputs are finite; a program needn't handle non-finite values.
Results may differ from the reference program's by a relative error of at most 0.0066.
Values may be sent and summed in bfloat16 or wider, within the bound.
A program may use at most 64 MiB of HBM per device.

```python
import math
import jax
import jax.numpy as jnp
from jax import lax

D = 4096
HD = 128
TD = 1536
PH = 1024
HALO = 8
TSTEPS = 1000
TOK_DEV = 64
S = 512
TT_DEV = 80
TT = 640
IMAGES = 8


def shared_keys(key):
    base = jax.random.truncated_normal(key, -4.5, 4.5, (IMAGES, S, D), jnp.float32)
    noise = jax.random.truncated_normal(jax.random.fold_in(key, 101), -4.5, 4.5, (IMAGES, S // 2, D), jnp.float32)
    chosen = jax.random.randint(jax.random.fold_in(key, 102), (IMAGES, S // 2), 0, 48) == 0
    even_rows = base[:, 0::2]
    odd_rows = jnp.where(chosen[:, :, None], even_rows + 0.2 * noise, base[:, 1::2])
    keyed = jnp.stack([even_rows, odd_rows], axis=2).reshape(IMAGES, S, D)
    return (keyed, even_rows, chosen)


def draw_keys(key, part):
    keyed, even_rows, chosen = shared_keys(key)
    return keyed.astype(jnp.bfloat16)


def draw_queries(key, part):
    keyed, even_rows, chosen = shared_keys(key)
    key = jax.random.fold_in(key, 7)
    own = jax.random.truncated_normal(key, -4.5, 4.5, (IMAGES, S, D), jnp.float32)
    strength_key = jax.random.fold_in(key, 8)
    strength = jax.random.uniform(strength_key, (IMAGES, S // 2), jnp.float32, 0.5, 1.5)
    even_own = jnp.where(chosen[:, :, None], strength[:, :, None] * even_rows, own[:, 0::2])
    joined = jnp.stack([even_own, own[:, 1::2]], axis=2).reshape(IMAGES, S, D)
    return joined.astype(jnp.bfloat16)


def draw_resample_index(key, part):
    key = jax.random.fold_in(key, 11)
    band = jnp.arange(S, dtype=jnp.int32) // TOK_DEV
    offset = jax.random.randint(key, (IMAGES, S, 4), -HALO, TT_DEV + HALO)
    index = band[None, :, None] * TT_DEV + offset
    return jnp.clip(index, 0, TT - 1).astype(jnp.int32)


def touch_ends(result, own_key, smallest, high):
    longest = result.shape.index(max(result.shape))
    spots = []
    for shift in (0, 1):
        where = [jax.random.randint(jax.random.fold_in(own_key, axis), (), 0, length) for axis, length in enumerate(result.shape)]
        where[longest] = (where[longest] + shift) % result.shape[longest]
        spots.append(tuple(where))
    return result.at[spots[0]].set(smallest).at[spots[1]].set(high)


def level_of(own_key, extent, shards, low, top_value):
    loudness, own = 1.0, jax.random.fold_in(own_key, 6)
    for axis_at, shards_of in shards:
        heights = jnp.exp(jax.random.uniform(jax.random.fold_in(own, axis_at), (shards_of,), jnp.float32, low / len(shards), top_value / len(shards)))
        loudness = loudness * jnp.repeat(heights, extent[axis_at] // shards_of).reshape([-1 if axis == axis_at else 1 for axis in range(len(extent))])
    return loudness


def bell_draw(stream_key, extent, width, bound, split=(), held_as=jnp.bfloat16):
    entries = jax.random.normal(stream_key, extent, jnp.float32) * width
    if len(split) > 0:
        entries = level_of(stream_key, extent, split, -0.22, 0.18) * entries
    return jnp.clip(entries, min=-bound, max=bound).astype(held_as)


def setup_inputs(seed: int = 0) -> dict:
    key_list = jax.random.split(jax.random.key(seed), 13)
    queries = draw_queries(jax.random.fold_in(key_list[12], 71), 0)
    keys = draw_keys(jax.random.fold_in(key_list[12], 71), 0)
    values = bell_draw(key_list[2], (IMAGES, S, D), 1.0, 6.0, ((0, 4), (1, 8)))
    teacher = bell_draw(key_list[3], (IMAGES, TT, TD), 1.0, 6.0, ((0, 4), (1, 8)))
    resample_index = draw_resample_index(jax.random.fold_in(key_list[12], 71), 0)
    resample_frac = touch_ends(jax.random.randint(key_list[5], (IMAGES, S, 2), 0, 8), jax.random.fold_in(key_list[5], 1), 0, 7).astype(jnp.int32)
    timesteps = touch_ends(jax.random.randint(key_list[6], (IMAGES,), 0, TSTEPS), jax.random.fold_in(key_list[6], 1), 0, TSTEPS - 1).astype(jnp.int32)
    norm_gain = jnp.clip(1.0 + 0.18 * jax.random.normal(key_list[7], (D,), jnp.float32), 0.1, 1.9)
    proj_in = bell_draw(key_list[8], (D, PH), D ** -0.5, 0.09375, ((0, 32),))
    bias_in = bell_draw(key_list[9], (PH,), 0.5, 3.0, (), jnp.float32)
    proj_out = bell_draw(key_list[10], (PH, TD), PH ** -0.5, 0.1875, ((0, 32),))
    bias_out = bell_draw(key_list[11], (TD,), 0.5, 3.0, (), jnp.float32)
    return dict(queries=queries, keys=keys, values=values, teacher=teacher, resample_index=resample_index, resample_frac=resample_frac, timesteps=timesteps, norm_gain=norm_gain, proj_in=proj_in, bias_in=bias_in, proj_out=proj_out, bias_out=bias_out)


epsilon = 1e-06
loss_scale = 256.0

def attend_image(query_img, key_img, value_img):
    head_count = D // HD
    query_heads = query_img.astype(jnp.float32).reshape(S, head_count, HD)
    key_heads = key_img.astype(jnp.float32).reshape(S, head_count, HD)
    value_heads = value_img.astype(jnp.float32).reshape(S, head_count, HD)
    scores = jnp.einsum('qhd,khd->hqk', query_heads, key_heads) * HD ** (-0.5)
    row_max = lax.optimization_barrier(jnp.max(scores, axis=-1, keepdims=True))
    exp_scores = jnp.exp(scores - row_max)
    row_total = lax.optimization_barrier(jnp.sum(exp_scores, axis=-1))
    prob_bf16 = exp_scores.astype(jnp.bfloat16)
    mixed_sum = jnp.einsum('hqk,khd->qhd', prob_bf16.astype(jnp.float32), value_heads)
    attended = mixed_sum / jnp.transpose(row_total)[:, :, None]
    return attended.reshape(S, D).astype(jnp.bfloat16)

def align_image(packed, norm_gain, proj_in, bias_in, proj_out, bias_out):
    query_img, key_img, value_img, teacher_img, index_img, frac_img, step_img = packed
    attended = attend_image(query_img, key_img, value_img)
    att_wide = attended.astype(jnp.float32)
    mean_square = lax.optimization_barrier(jnp.mean(att_wide * att_wide, axis=-1, keepdims=True))
    inv_rms = lax.rsqrt(mean_square + epsilon)
    normed = (att_wide * inv_rms * norm_gain).astype(jnp.bfloat16)
    pre_act = jnp.dot(normed, proj_in, preferred_element_type=jnp.float32) + bias_in
    hidden = jax.nn.silu(pre_act).astype(jnp.bfloat16)
    projected = jnp.dot(hidden, proj_out, preferred_element_type=jnp.float32) + bias_out
    frac_x = frac_img[:, 0].astype(jnp.float32)
    frac_y = frac_img[:, 1].astype(jnp.float32)
    stencil = jnp.stack([(8.0 - frac_x) * (8.0 - frac_y), frac_x * (8.0 - frac_y), (8.0 - frac_x) * frac_y, frac_x * frac_y], axis=-1) / 64.0
    picked = jnp.take(teacher_img, index_img.reshape(-1).astype(jnp.int32), axis=0)
    picked = picked.reshape(S, 4, TD).astype(jnp.float32)
    target = lax.optimization_barrier(jnp.sum(stencil[:, :, None] * picked, axis=1))
    proj_norm = jnp.sqrt(lax.optimization_barrier(jnp.sum(projected * projected, axis=-1, keepdims=True)) + epsilon)
    target_norm = jnp.sqrt(lax.optimization_barrier(jnp.sum(target * target, axis=-1, keepdims=True)) + epsilon)
    alignment = lax.optimization_barrier(jnp.sum(projected * target, axis=-1, keepdims=True)) / (proj_norm * target_norm)
    time_weight = 0.25 + 0.75 * jnp.cos(0.5 * math.pi * step_img.astype(jnp.float32) / TSTEPS) ** 2
    d_projected = -loss_scale * time_weight * (target / (proj_norm * target_norm) - alignment * projected / (proj_norm * proj_norm))
    d_proj_bf = d_projected.astype(jnp.bfloat16)
    d_hidden = jnp.dot(d_proj_bf, proj_out.T, preferred_element_type=jnp.float32)
    gate_sig = jax.nn.sigmoid(pre_act)
    d_pre = (d_hidden * gate_sig * (1.0 + pre_act * (1.0 - gate_sig))).astype(jnp.bfloat16)
    d_normed = jnp.dot(d_pre, proj_in.T, preferred_element_type=jnp.float32)
    gained = d_normed * norm_gain
    cubed = inv_rms * inv_rms * inv_rms
    grad_att = inv_rms * gained - att_wide * cubed * lax.optimization_barrier(jnp.mean(att_wide * gained, axis=-1, keepdims=True))
    return (alignment[:, 0], grad_att.astype(jnp.bfloat16))

def reference(queries, keys, values, teacher, resample_index, resample_frac, timesteps, norm_gain, proj_in, bias_in, proj_out, bias_out):

    def per_image(packed):
        return align_image(packed, norm_gain, proj_in, bias_in, proj_out, bias_out)
    alignment, grad_attended = lax.map(per_image, (queries, keys, values, teacher, resample_index, resample_frac, timesteps))
    return (alignment, grad_attended)
```

```python
import functools
import math

import jax
import jax.numpy as jnp
from jax import lax
from jax.experimental import pallas as pl
from jax.experimental.pallas import tpu as pltpu
from jax.sharding import PartitionSpec as P

HD = 128
HALO = 16
TSTEPS = 1000
MESH = pl.DeviceIdType.MESH

epsilon = 1e-06
loss_scale = 256.0
NT = (((1,), (1,)), ((), ()))


def attend_kernel(
    n, chunk, q_ref, k_ref, v_ref, t_ref, idx_ref, frac_ref, att_ref, target_ref,
    held, mixed, halo, send_sem, recv_sem, back_send, back_recv, halo_send, halo_recv,
):
    dp, me = lax.axis_index("dp"), lax.axis_index("seq")
    images, rows, width = q_ref.shape
    local = width // n
    chunks = local // chunk
    length = rows * n
    band = t_ref.shape[1]
    right, left = lax.rem(me + 1, n), lax.rem(me + n - 1, n)

    barrier = pltpu.get_barrier_semaphore()

    @pl.loop(1, n)
    def _(step):
        pl.semaphore_signal(
            barrier, inc=1, device_id=(dp, lax.rem(me + step, n)), device_id_type=MESH
        )

    pl.semaphore_wait(barrier, n - 1)

    sources = (q_ref, k_ref, v_ref)
    my_rows = pl.ds(pl.multiple_of(me * rows, rows), rows)

    def columns(owner, part):
        return pl.ds(pl.multiple_of(owner * local + part * chunk, chunk), chunk)

    halo_copies = [
        pltpu.make_async_remote_copy(
            src_ref=t_ref.at[:, pl.ds(start, HALO), :],
            dst_ref=halo.at[side],
            send_sem=halo_send.at[side],
            recv_sem=halo_recv.at[side],
            device_id=(dp, to),
            device_id_type=MESH,
        )
        for side, start, to in ((0, band - HALO, right), (1, 0, left))
    ]
    for copy in halo_copies:
        copy.start()
    for image in range(images):
        for part in range(chunks):
            for which, source in enumerate(sources):
                pltpu.make_async_copy(
                    source.at[image, :, columns(me, part)],
                    held.at[which, image, part, my_rows, :],
                    recv_sem.at[which, image, part],
                ).start()

                @pl.loop(1, n)
                def _(step, source=source, which=which, image=image, part=part):
                    to = lax.rem(me + step, n)
                    pltpu.make_async_remote_copy(
                        src_ref=source.at[image, :, columns(to, part)],
                        dst_ref=held.at[which, image, part, my_rows, :],
                        send_sem=send_sem.at[which],
                        recv_sem=recv_sem.at[which, image, part],
                        device_id=(dp, to),
                        device_id_type=MESH,
                    ).start()

    for copy in halo_copies:
        copy.wait()
    reach = band + 2 * HALO
    lane = lax.broadcasted_iota(jnp.int32, (rows, reach), 1) + (me * band - HALO)
    for image in range(images):
        index, frac = idx_ref[image], frac_ref[image].astype(jnp.float32)
        fx, fy = frac[:, 0:1], frac[:, 1:2]
        weights = ((8.0 - fx) * (8.0 - fy), fx * (8.0 - fy), (8.0 - fx) * fy, fx * fy)
        spread = jnp.zeros((rows, reach), jnp.float32)
        for j in range(4):
            spread += jnp.where(index[:, j : j + 1] == lane, weights[j], 0.0)
        spread = (spread * (1.0 / 64.0)).astype(jnp.bfloat16)
        before = jnp.where(me > 0, halo[0, image], jnp.zeros_like(halo[0, image]))
        after = jnp.where(me < n - 1, halo[1, image], jnp.zeros_like(halo[1, image]))
        near = jnp.concatenate([before, t_ref[image], after], axis=0)
        target_ref[pl.ds(image * rows, rows), :] = jnp.dot(
            spread, near, preferred_element_type=jnp.float32
        )

    block = min(length, 512)
    scale = HD ** (-0.5)
    for image in range(images):
        for part in range(chunks):
            for which in range(3):
                full = held.at[which, image, part]
                pltpu.make_async_copy(full, full, recv_sem.at[which, image, part]).wait()
            for head in range(chunk // HD):
                cols = pl.ds(head * HD, HD)
                key = held[1, image, part, :, cols]
                value = held[2, image, part, :, cols]
                for at in range(0, length, block):
                    query = held[0, image, part, pl.ds(at, block), cols]
                    scores = lax.dot_general(query, key, NT, preferred_element_type=jnp.float32)
                    top = jnp.max(scores, axis=-1, keepdims=True)
                    prob = jnp.exp((scores - top) * scale)
                    total = jnp.sum(prob, axis=-1, keepdims=True)
                    out = jnp.dot(
                        prob.astype(jnp.bfloat16), value, preferred_element_type=jnp.float32
                    )
                    mixed[image, part, pl.ds(at, block), cols] = (out / total).astype(jnp.bfloat16)
            pltpu.make_async_copy(
                mixed.at[image, part, my_rows, :],
                att_ref.at[image, :, columns(me, part)],
                back_recv,
            ).start()

            @pl.loop(1, n)
            def _(step, image=image, part=part):
                to = lax.rem(me + step, n)
                pltpu.make_async_remote_copy(
                    src_ref=mixed.at[image, part, pl.ds(pl.multiple_of(to * rows, rows), rows), :],
                    dst_ref=att_ref.at[image, :, columns(me, part)],
                    send_sem=back_send,
                    recv_sem=back_recv,
                    device_id=(dp, to),
                    device_id_type=MESH,
                ).start()

    for which, source in enumerate(sources):
        sent = source.at[:, :, pl.ds(0, width - local)]
        pltpu.make_async_copy(sent, sent, send_sem.at[which]).wait()
    sent = mixed.at[:, :, pl.ds(0, length - rows), :]
    pltpu.make_async_copy(sent, sent, back_send).wait()
    pltpu.make_async_copy(att_ref, att_ref, back_recv).wait()


def attend(n, queries, keys, values, teacher, index, frac):
    images, rows, width = queries.shape
    local = width // n
    chunk = min(local, 2 * HD)
    chunks = local // chunk
    length = rows * n
    vmem = pl.BlockSpec(memory_space=pltpu.VMEM)
    hbm = pl.BlockSpec(memory_space=pl.ANY)
    dma = pltpu.SemaphoreType.DMA
    return pl.pallas_call(
        functools.partial(attend_kernel, n, chunk),
        out_shape=(
            jax.ShapeDtypeStruct(queries.shape, jnp.bfloat16),
            jax.ShapeDtypeStruct((images * rows, teacher.shape[2]), jnp.float32),
        ),
        in_specs=[hbm, hbm, hbm, vmem, vmem, vmem],
        out_specs=(hbm, vmem),
        scratch_shapes=[
            pltpu.VMEM((3, images, chunks, length, chunk), jnp.bfloat16),
            pltpu.VMEM((images, chunks, length, chunk), jnp.bfloat16),
            pltpu.VMEM((2, images, HALO, teacher.shape[2]), jnp.bfloat16),
            dma((3,)),
            dma((3, images, chunks)),
            dma,
            dma,
            dma((2,)),
            dma((2,)),
        ],
        compiler_params=pltpu.CompilerParams(
            collective_id=0, has_side_effects=True, vmem_limit_bytes=40 * 2**20
        ),
        cost_estimate=pl.CostEstimate(
            flops=4 * images * length * length * local,
            bytes_accessed=300 * 2**20,
            transcendentals=images * length * length * local // HD,
        ),
        name="attend",
    )(queries, keys, values, teacher, index, frac)


def project_kernel(
    att_ref, target_ref, tw_ref, gain_ref, bias_in_ref, bias_out_ref, in_hbm, out_hbm,
    align_ref, grad_ref, in_ref, out_ref, in_sem, out_sem,
):
    images, rows, width = att_ref.shape
    total = images * rows
    depth = in_hbm.shape[0] // in_sem.shape[0]
    count = in_sem.shape[0]

    in_copies = [
        pltpu.make_async_copy(
            in_hbm.at[pl.ds(c * depth, depth), :], in_ref.at[pl.ds(c * depth, depth), :], in_sem.at[c]
        )
        for c in range(count)
    ]
    out_copy = pltpu.make_async_copy(out_hbm, out_ref, out_sem)
    for copy in in_copies:
        copy.start()
    out_copy.start()

    def attended(c):
        return att_ref[:, :, pl.ds(c * depth, depth)].reshape(total, depth).astype(jnp.float32)

    squares = jnp.zeros((total, 1), jnp.float32)
    for c in range(count):
        wide = attended(c)
        squares += jnp.sum(wide * wide, axis=-1, keepdims=True)
    inv_rms = lax.rsqrt(squares / width + epsilon)

    raw = jnp.zeros((total, in_hbm.shape[1]), jnp.float32)
    for c in range(count):
        normed = (attended(c) * inv_rms * gain_ref[:, pl.ds(c * depth, depth)]).astype(jnp.bfloat16)
        in_copies[c].wait()
        raw += jnp.dot(
            normed, in_ref[pl.ds(c * depth, depth), :], preferred_element_type=jnp.float32
        )
    pre_act = raw + bias_in_ref[...]
    gate = 1.0 / (1.0 + jnp.exp(-pre_act))
    hidden = (pre_act * gate).astype(jnp.bfloat16)
    out_copy.wait()
    projected = (
        jnp.dot(hidden, out_ref[...], preferred_element_type=jnp.float32) + bias_out_ref[...]
    )
    target = target_ref[...]
    pp = jnp.sum(projected * projected, axis=-1, keepdims=True) + epsilon
    tt = jnp.sum(target * target, axis=-1, keepdims=True) + epsilon
    pt = jnp.sum(projected * target, axis=-1, keepdims=True)
    both = lax.rsqrt(pp) * lax.rsqrt(tt)
    alignment = pt * both
    spread = jnp.transpose(jnp.broadcast_to(alignment, (total, 128)))
    for image in range(images):
        align_ref[image : image + 1, :] = spread[0:1, image * rows : (image + 1) * rows]
    factor = -loss_scale * tw_ref[...]
    d_proj = (factor * both * target - (factor * alignment / pp) * projected).astype(jnp.bfloat16)
    d_hidden = lax.dot_general(d_proj, out_ref[...], NT, preferred_element_type=jnp.float32)
    d_pre = (d_hidden * gate * (1.0 + pre_act * (1.0 - gate))).astype(jnp.bfloat16)
    mean = jnp.sum(d_pre.astype(jnp.float32) * raw, axis=-1, keepdims=True) / (inv_rms * width)
    pull = inv_rms * inv_rms * inv_rms * mean
    for c in range(count):
        cols = pl.ds(c * depth, depth)
        d_normed = lax.dot_general(
            d_pre, in_ref[cols, :], NT, preferred_element_type=jnp.float32
        )
        grad = inv_rms * gain_ref[:, cols] * d_normed - attended(c) * pull
        grad_ref[:, :, cols] = grad.astype(jnp.bfloat16).reshape(images, rows, depth)


def project(att, target, time_weight, gain, bias_in, bias_out, full_in, full_out):
    images, rows, width = att.shape
    vmem = pl.BlockSpec(memory_space=pltpu.VMEM)
    hbm = pl.BlockSpec(memory_space=pl.ANY)
    dma = pltpu.SemaphoreType.DMA
    return pl.pallas_call(
        project_kernel,
        out_shape=(
            jax.ShapeDtypeStruct((images, rows), jnp.float32),
            jax.ShapeDtypeStruct(att.shape, jnp.bfloat16),
        ),
        in_specs=[vmem] * 6 + [hbm, hbm],
        out_specs=(vmem, vmem),
        scratch_shapes=[
            pltpu.VMEM(full_in.shape, jnp.bfloat16),
            pltpu.VMEM(full_out.shape, jnp.bfloat16),
            dma((8,)),
            dma,
        ],
        compiler_params=pltpu.CompilerParams(vmem_limit_bytes=40 * 2**20),
        name="project",
    )(att, target, time_weight, gain, bias_in, bias_out, full_in, full_out)


def shards(
    queries,
    keys,
    values,
    teacher,
    resample_index,
    resample_frac,
    timesteps,
    norm_gain,
    proj_in,
    bias_in,
    proj_out,
    bias_out,
):
    rows = queries.shape[1]
    full_in = lax.all_gather(proj_in, ("dp", "seq"), axis=0, tiled=True)
    full_out = lax.all_gather(proj_out, ("dp", "seq"), axis=0, tiled=True)
    image_weight = (
        0.25 + 0.75 * jnp.cos(0.5 * math.pi * timesteps.astype(jnp.float32) / TSTEPS) ** 2
    )
    time_weight = jnp.repeat(image_weight, rows)[:, None]
    att, target = attend(
        lax.axis_size("seq"), queries, keys, values, teacher, resample_index, resample_frac
    )
    return project(
        att, target, time_weight, norm_gain[None], bias_in[None], bias_out[None], full_in, full_out
    )


def solution(mesh):
    return jax.shard_map(
        shards,
        mesh=mesh,
        in_specs=(
            P("dp", "seq", None),
            P("dp", "seq", None),
            P("dp", "seq", None),
            P("dp", "seq", None),
            P("dp", "seq", None),
            P("dp", "seq", None),
            P("dp"),
            P(),
            P(("dp", "seq"), None),
            P(),
            P(("dp", "seq"), None),
            P(),
        ),
        out_specs=(P("dp", "seq"), P("dp", "seq", None)),
        check_vma=False,
    )
```

```python
import functools
import math

import jax
import jax.numpy as jnp
from jax import lax
from jax.experimental import pallas as pl
from jax.experimental.pallas import tpu as pltpu
from jax.sharding import PartitionSpec as P

HD = 128
HALO = 16
TSTEPS = 1000
MESH = pl.DeviceIdType.MESH

epsilon = 1e-06
loss_scale = 256.0
NT = (((1,), (1,)), ((), ()))


def align_kernel(
    n, chunk, gather,
    q_ref, k_ref, v_ref, t_ref, idx_ref, frac_ref, step_ref, gain_hbm, bias_in_hbm, bias_out_hbm,
    in_hbm, out_hbm,
    align_ref, grad_ref,
    held, mixed, att_ref, target_ref, near, in_ref, out_ref, gain_ref, bias_in_ref, bias_out_ref,
    send_sem, recv_sem, back_send, back_recv, halo_send, halo_recv, near_sem, small_sem,
    w_local, w_recv, line_send, side_send,
):
    dp, me = lax.axis_index("dp"), lax.axis_index("seq")
    images, rows, width = q_ref.shape
    total = images * rows
    local = width // n
    chunks = local // chunk
    length = rows * n
    band = t_ref.shape[1]
    reach = band + 2 * HALO
    right, left = lax.rem(me + 1, n), lax.rem(me + n - 1, n)
    here = dp * n + me
    weights = ((in_ref, in_hbm.shape[0]), (out_ref, out_hbm.shape[0]))

    def piece(j, block, count=1):
        ref, size = weights[j]
        return ref.at[pl.ds(pl.multiple_of(block * size, size), count * size), :]

    own = here if gather else 0
    w_copies = [
        pltpu.make_async_copy(source, piece(j, own), w_local.at[j])
        for j, source in enumerate((in_hbm, out_hbm))
    ]
    near_copy = pltpu.make_async_copy(t_ref, near.at[:, pl.ds(HALO, band), :], near_sem)
    small_copies = [
        pltpu.make_async_copy(source, dest, small_sem.at[j])
        for j, (source, dest) in enumerate(
            ((gain_hbm, gain_ref), (bias_in_hbm, bias_in_ref), (bias_out_hbm, bias_out_ref))
        )
    ]
    for copy in w_copies + [near_copy] + small_copies:
        copy.start()

    barrier = pltpu.get_barrier_semaphore()

    @pl.loop(1, n)
    def _(step):
        pl.semaphore_signal(
            barrier, inc=1, device_id=(dp, lax.rem(me + step, n)), device_id_type=MESH
        )

    greeted = n - 1
    if gather:
        core, y = lax.rem(dp, 2), lax.div(dp, 2)
        x, z = lax.rem(me, 2), lax.div(me, 2)
        lines = n // 2
        sibling = (y * 2 + (1 - core), me)
        across_y = ((1 - y) * 2 + core, me)
        across_x = (dp, z * 2 + (1 - x))
        for partner in (sibling, across_y):
            pl.semaphore_signal(barrier, inc=1, device_id=partner, device_id_type=MESH)
        greeted += 2
    pl.semaphore_wait(barrier, greeted)

    def push(block, device, sems):
        for j in range(2):
            pltpu.make_async_remote_copy(
                src_ref=piece(j, block),
                dst_ref=piece(j, block),
                send_sem=sems[j],
                recv_sem=w_recv.at[j, block],
                device_id=device,
                device_id_type=MESH,
            ).start()

    def arrived(block):
        for j in range(2):
            pltpu.make_async_copy(piece(j, block), piece(j, block), w_recv.at[j, block]).wait()

    def line_sems(side, step):
        return [line_send.at[side, step, j] for j in range(2)]

    def side_sems(kind):
        return [side_send.at[kind, j] for j in range(2)]

    def block_at(y_of, core_of, z_of, x_of):
        return (y_of * 2 + core_of) * n + z_of * 2 + x_of

    def spread_from_line(block):
        push(block, across_y, side_sems(1))
        push(block, across_x, side_sems(0))
        push(block, sibling, side_sems(2))

    def at_distance(step, act):
        if step == 0:
            act(z, 0)
            return

        @pl.when(z - step >= 0)
        def _():
            act(z - step, 1)

        @pl.when(z + step < lines)
        def _():
            act(z + step, 2)

    def go_on(step, z_of, come_from):
        block = block_at(y, core, z_of, x)
        if come_from != 0:
            arrived(block)
        if come_from != 2:
            @pl.when(z + 1 < lines)
            def _():
                push(block, (dp, me + 2), line_sems(0, step))
        if come_from != 1:
            @pl.when(z >= 1)
            def _():
                push(block, (dp, me - 2), line_sems(1, step))
        spread_from_line(block)

    def line_stage(step):
        at_distance(step, lambda z_of, side: go_on(step, z_of, side))

    def x_stage(step):
        def act(z_of, side):
            block = block_at(y, core, z_of, 1 - x)
            arrived(block)
            push(block, across_y, side_sems(1))
            push(block, sibling, side_sems(2))

        at_distance(step, act)

    def y_stage(step):
        def act(z_of, side):
            for x_of in (x, 1 - x):
                block = block_at(1 - y, core, z_of, x_of)
                arrived(block)
                push(block, sibling, side_sems(2))

        at_distance(step, act)

    def weight_stage(slot):
        if not gather:
            return
        if slot < lines:
            line_stage(slot)
        if 1 <= slot <= lines:
            x_stage(slot - 1)
        if 3 <= slot <= lines + 2:
            y_stage(slot - 3)

    sources = (q_ref, k_ref, v_ref)
    my_rows = pl.ds(pl.multiple_of(me * rows, rows), rows)

    def columns(owner, part):
        return pl.ds(pl.multiple_of(owner * local + part * chunk, chunk), chunk)

    work = [(image, part) for image in range(images) for part in range(chunks)]

    def issue(at):
        if at >= len(work):
            return
        image, part = work[at]
        for which, source in enumerate(sources):
            pltpu.make_async_copy(
                source.at[image, :, columns(me, part)],
                held.at[which, image, part, my_rows, :],
                recv_sem.at[which, image, part],
            ).start()

        @pl.loop(1, n)
        def _(step):
            to = lax.rem(me + step, n)
            for which, source in enumerate(sources):
                pltpu.make_async_remote_copy(
                    src_ref=source.at[image, :, columns(to, part)],
                    dst_ref=held.at[which, image, part, my_rows, :],
                    send_sem=send_sem.at[which],
                    recv_sem=recv_sem.at[which, image, part],
                    device_id=(dp, to),
                    device_id_type=MESH,
                ).start()

    halo_copies = [
        pltpu.make_async_remote_copy(
            src_ref=t_ref.at[:, pl.ds(start, HALO), :],
            dst_ref=near.at[:, pl.ds(land, HALO), :],
            send_sem=halo_send.at[side],
            recv_sem=halo_recv.at[side],
            device_id=(dp, to),
            device_id_type=MESH,
        )
        for side, start, land, to in ((0, band - HALO, 0, right), (1, 0, band + HALO, left))
    ]
    for copy in w_copies:
        if gather:
            copy.wait()
    for copy in halo_copies:
        copy.start()
    weight_stage(0)
    issue(0)

    near_copy.wait()
    for copy in halo_copies:
        copy.wait()
    row = lax.broadcasted_iota(jnp.int32, (reach, rows), 0) + (me * band - HALO)
    real = lax.broadcasted_iota(jnp.int32, (reach, near.shape[2]), 0) + (me * band - HALO)
    real = jnp.logical_and(real >= 0, real < n * band)
    for image in range(images):
        index, frac = idx_ref[image], frac_ref[image].astype(jnp.float32)
        fx, fy = frac[0:1, :], frac[1:2, :]
        factors = ((8.0 - fx) * (8.0 - fy), fx * (8.0 - fy), (8.0 - fx) * fy, fx * fy)
        spread = jnp.zeros((reach, rows), jnp.float32)
        for j in range(4):
            spread += jnp.where(index[j : j + 1, :] == row, factors[j], 0.0)
        spread = (spread * (1.0 / 64.0)).astype(jnp.bfloat16)
        wide = jnp.where(real, near[image].astype(jnp.float32), 0.0).astype(jnp.bfloat16)
        target_ref[pl.ds(image * rows, rows), :] = lax.dot_general(
            spread, wide, (((0,), (0,)), ((), ())), preferred_element_type=jnp.float32
        )
    weight_stage(1)
    issue(1)

    block_rows = min(length, 512)
    scale = HD ** (-0.5)
    for at, (image, part) in enumerate(work):
        for which in range(3):
            full = held.at[which, image, part]
            pltpu.make_async_copy(full, full, recv_sem.at[which, image, part]).wait()
        issue(at + 2)
        for head in range(chunk // HD):
            cols = pl.ds(head * HD, HD)
            key = held[1, image, part, :, cols]
            value = held[2, image, part, :, cols]
            for start in range(0, length, block_rows):
                query = held[0, image, part, pl.ds(start, block_rows), cols]
                scores = lax.dot_general(query, key, NT, preferred_element_type=jnp.float32)
                top = jnp.max(scores, axis=-1, keepdims=True)
                prob = jnp.exp((scores - top) * scale)
                mass = jnp.sum(prob, axis=-1, keepdims=True)
                out = jnp.dot(prob.astype(jnp.bfloat16), value, preferred_element_type=jnp.float32)
                mixed[image, part, pl.ds(start, block_rows), cols] = (out / mass).astype(
                    jnp.bfloat16
                )
        pltpu.make_async_copy(
            mixed.at[image, part, my_rows, :], att_ref.at[image, :, columns(me, part)], back_recv
        ).start()

        @pl.loop(1, n)
        def _(step, image=image, part=part):
            to = lax.rem(me + step, n)
            pltpu.make_async_remote_copy(
                src_ref=mixed.at[image, part, pl.ds(pl.multiple_of(to * rows, rows), rows), :],
                dst_ref=att_ref.at[image, :, columns(me, part)],
                send_sem=back_send,
                recv_sem=back_recv,
                device_id=(dp, to),
                device_id_type=MESH,
            ).start()

        weight_stage(at + 2)

    if gather:
        for slot in range(len(work) + 2, lines + 3):
            weight_stage(slot)
    pltpu.make_async_copy(att_ref, att_ref, back_recv).wait()

    for copy in small_copies:
        copy.wait()
    if gather:
        @pl.loop(0, n)
        def _(at):
            for y_of in range(2):
                arrived((y_of * 2 + (1 - core)) * n + at)
    else:
        for copy in w_copies:
            copy.wait()

    depth = in_ref.shape[0] // 8

    def attended(c):
        return att_ref[:, :, pl.ds(c * depth, depth)].reshape(total, depth).astype(jnp.float32)

    squares = jnp.zeros((total, 1), jnp.float32)
    for c in range(8):
        wide = attended(c)
        squares += jnp.sum(wide * wide, axis=-1, keepdims=True)
    inv_rms = lax.rsqrt(squares / width + epsilon)

    raw = jnp.zeros((total, in_ref.shape[1]), jnp.float32)
    for c in range(8):
        normed = (attended(c) * inv_rms * gain_ref[:, pl.ds(c * depth, depth)]).astype(jnp.bfloat16)
        raw += jnp.dot(
            normed, in_ref[pl.ds(c * depth, depth), :], preferred_element_type=jnp.float32
        )
    pre_act = raw + bias_in_ref[...]
    gate = 1.0 / (1.0 + jnp.exp(-pre_act))
    hidden = (pre_act * gate).astype(jnp.bfloat16)
    projected = (
        jnp.dot(hidden, out_ref[...], preferred_element_type=jnp.float32) + bias_out_ref[...]
    )
    target = target_ref[...]
    pp = jnp.sum(projected * projected, axis=-1, keepdims=True) + epsilon
    tt = jnp.sum(target * target, axis=-1, keepdims=True) + epsilon
    pt = jnp.sum(projected * target, axis=-1, keepdims=True)
    both = lax.rsqrt(pp) * lax.rsqrt(tt)
    alignment = pt * both
    turned = jnp.transpose(jnp.broadcast_to(alignment, (total, 128)))
    for image in range(images):
        align_ref[image : image + 1, :] = turned[0:1, image * rows : (image + 1) * rows]
    steps = jnp.concatenate(
        [jnp.full((rows, 1), step_ref[image], jnp.int32) for image in range(images)], axis=0
    )
    wave = jnp.cos(0.5 * math.pi * steps.astype(jnp.float32) / TSTEPS)
    factor = -loss_scale * (0.25 + 0.75 * wave * wave)
    d_proj = (factor * both * target - (factor * alignment / pp) * projected).astype(jnp.bfloat16)
    d_hidden = lax.dot_general(d_proj, out_ref[...], NT, preferred_element_type=jnp.float32)
    d_pre = (d_hidden * gate * (1.0 + pre_act * (1.0 - gate))).astype(jnp.bfloat16)
    mean = jnp.sum(d_pre.astype(jnp.float32) * raw, axis=-1, keepdims=True) / (inv_rms * width)
    pull = inv_rms * inv_rms * inv_rms * mean
    for c in range(8):
        cols = pl.ds(c * depth, depth)
        d_normed = lax.dot_general(d_pre, in_ref[cols, :], NT, preferred_element_type=jnp.float32)
        grad = inv_rms * gain_ref[:, cols] * d_normed - attended(c) * pull
        grad_ref[:, :, cols] = grad.astype(jnp.bfloat16).reshape(images, rows, depth)

    for which, source in enumerate(sources):
        sent = source.at[:, :, pl.ds(0, width - local)]
        pltpu.make_async_copy(sent, sent, send_sem.at[which]).wait()
    sent = mixed.at[:, :, pl.ds(0, length - rows), :]
    pltpu.make_async_copy(sent, sent, back_send).wait()
    if gather:
        for kind, count in ((0, lines), (1, n), (2, 2 * n)):
            for j in range(2):
                sent = piece(j, 0, count)
                pltpu.make_async_copy(sent, sent, side_send.at[kind, j]).wait()

        def line_left(side, step, there):
            @pl.when(there)
            def _():
                for j in range(2):
                    sent = piece(j, 0)
                    pltpu.make_async_copy(sent, sent, line_send.at[side, step, j]).wait()

        for step in range(lines):
            line_left(0, step, jnp.logical_and(z - step >= 0, z + 1 < lines))
            line_left(1, step, jnp.logical_and(z + step < lines, z >= 1))


def shards(
    queries,
    keys,
    values,
    teacher,
    resample_index,
    resample_frac,
    timesteps,
    norm_gain,
    proj_in,
    bias_in,
    proj_out,
    bias_out,
):
    n, planes = lax.axis_size("seq"), lax.axis_size("dp")
    images, rows, width = queries.shape
    features = teacher.shape[2]
    hidden = proj_in.shape[1]
    gather = planes == 4 and n % 2 == 0 and proj_in.shape[0] % 16 == 0 and proj_out.shape[0] % 16 == 0
    if not gather:
        proj_in = lax.all_gather(proj_in, ("dp", "seq"), axis=0, tiled=True)
        proj_out = lax.all_gather(proj_out, ("dp", "seq"), axis=0, tiled=True)
    local = width // n
    chunk = min(local, 2 * HD)
    chunks = local // chunk
    length = rows * n
    band = teacher.shape[1]
    vmem = pl.BlockSpec(memory_space=pltpu.VMEM)
    smem = pl.BlockSpec(memory_space=pltpu.SMEM)
    hbm = pl.BlockSpec(memory_space=pl.ANY)
    dma = pltpu.SemaphoreType.DMA
    bf16, f32 = jnp.bfloat16, jnp.float32
    return pl.pallas_call(
        functools.partial(align_kernel, n, chunk, gather),
        out_shape=(
            jax.ShapeDtypeStruct((images, rows), f32),
            jax.ShapeDtypeStruct(queries.shape, bf16),
        ),
        in_specs=[hbm, hbm, hbm, hbm, vmem, vmem, smem, hbm, hbm, hbm, hbm, hbm],
        out_specs=(vmem, vmem),
        scratch_shapes=[
            pltpu.VMEM((3, images, chunks, length, chunk), bf16),
            pltpu.VMEM((images, chunks, length, chunk), bf16),
            pltpu.VMEM(queries.shape, bf16),
            pltpu.VMEM((images * rows, features), f32),
            pltpu.VMEM((images, band + 2 * HALO, features), bf16),
            pltpu.VMEM((width, hidden), bf16),
            pltpu.VMEM((hidden, features), bf16),
            pltpu.VMEM((1, width), f32),
            pltpu.VMEM((1, hidden), f32),
            pltpu.VMEM((1, features), f32),
            dma((3,)),
            dma((3, images, chunks)),
            dma,
            dma,
            dma((2,)),
            dma((2,)),
            dma,
            dma((3,)),
            dma((2,)),
            dma((2, planes * n if gather else 1)),
            dma((2, max(n // 2, 1), 2)),
            dma((3, 2)),
        ],
        compiler_params=pltpu.CompilerParams(
            collective_id=0, has_side_effects=True, vmem_limit_bytes=52 * 2**20
        ),
        name="align",
    )(
        queries, keys, values, teacher,
        jnp.transpose(resample_index, (0, 2, 1)), jnp.transpose(resample_frac, (0, 2, 1)),
        timesteps, norm_gain[None], bias_in[None], bias_out[None], proj_in, proj_out,
    )


def solution(mesh):
    return jax.shard_map(
        shards,
        mesh=mesh,
        in_specs=(
            P("dp", "seq", None),
            P("dp", "seq", None),
            P("dp", "seq", None),
            P("dp", "seq", None),
            P("dp", "seq", None),
            P("dp", "seq", None),
            P("dp"),
            P(),
            P(("dp", "seq"), None),
            P(),
            P(("dp", "seq"), None),
            P(),
        ),
        out_specs=(P("dp", "seq"), P("dp", "seq", None)),
        check_vma=False,
    )
```

```python
import functools
import math

import jax
import jax.numpy as jnp
from jax import lax
from jax.experimental import pallas as pl
from jax.experimental.pallas import tpu as pltpu
from jax.sharding import PartitionSpec as P

HD = 128
HALO = 16
TSTEPS = 1000
MESH = pl.DeviceIdType.MESH

epsilon = 1e-06
loss_scale = 256.0
NT = (((1,), (1,)), ((), ()))


def align_kernel(
    n, chunk, gather,
    q_ref, k_ref, v_ref, t_ref, idx_ref, frac_ref, step_ref, gain_hbm, bias_in_hbm, bias_out_hbm,
    in_hbm, out_hbm,
    align_ref, grad_ref,
    held, mixed, att_ref, target_ref, near, in_ref, out_ref, gain_ref, bias_in_ref, bias_out_ref,
    send_sem, recv_sem, back_send, back_recv, halo_send, halo_recv, near_sem, small_sem,
    w_local, w_recv, line_send, side_send,
):
    dp, me = lax.axis_index("dp"), lax.axis_index("seq")
    images, rows, width = q_ref.shape
    total = images * rows
    local = width // n
    chunks = local // chunk
    length = rows * n
    band = t_ref.shape[1]
    reach = band + 2 * HALO
    right, left = lax.rem(me + 1, n), lax.rem(me + n - 1, n)

    def peer(step):
        return lax.bitwise_xor(me, step) if n & (n - 1) == 0 else lax.rem(me + step, n)

    here = dp * n + me
    weights = ((in_ref, in_hbm.shape[0]), (out_ref, out_hbm.shape[0]))

    def piece(j, block, count=1):
        ref, size = weights[j]
        return ref.at[pl.ds(pl.multiple_of(block * size, size), count * size), :]

    own = here if gather else 0
    w_copies = [
        pltpu.make_async_copy(source, piece(j, own), w_local.at[j])
        for j, source in enumerate((in_hbm, out_hbm))
    ]
    near_copy = pltpu.make_async_copy(t_ref, near.at[:, pl.ds(HALO, band), :], near_sem)
    small_copies = [
        pltpu.make_async_copy(source, dest, small_sem.at[j])
        for j, (source, dest) in enumerate(
            ((gain_hbm, gain_ref), (bias_in_hbm, bias_in_ref), (bias_out_hbm, bias_out_ref))
        )
    ]
    for copy in w_copies + [near_copy] + small_copies:
        copy.start()

    barrier = pltpu.get_barrier_semaphore()

    @pl.loop(1, n)
    def _(step):
        pl.semaphore_signal(
            barrier, inc=1, device_id=(dp, lax.rem(me + step, n)), device_id_type=MESH
        )

    greeted = n - 1
    if gather:
        core, y = lax.rem(dp, 2), lax.div(dp, 2)
        x, z = lax.rem(me, 2), lax.div(me, 2)
        lines = n // 2
        sibling = (y * 2 + (1 - core), me)
        across_y = ((1 - y) * 2 + core, me)
        across_x = (dp, z * 2 + (1 - x))
        for partner in (sibling, across_y):
            pl.semaphore_signal(barrier, inc=1, device_id=partner, device_id_type=MESH)
        greeted += 2
    pl.semaphore_wait(barrier, greeted)

    def push(block, device, sems):
        for j in range(2):
            pltpu.make_async_remote_copy(
                src_ref=piece(j, block),
                dst_ref=piece(j, block),
                send_sem=sems[j],
                recv_sem=w_recv.at[j, block],
                device_id=device,
                device_id_type=MESH,
            ).start()

    def arrived(block):
        for j in range(2):
            pltpu.make_async_copy(piece(j, block), piece(j, block), w_recv.at[j, block]).wait()

    def line_sems(side, step):
        return [line_send.at[side, step, j] for j in range(2)]

    def side_sems(kind):
        return [side_send.at[kind, j] for j in range(2)]

    def block_at(y_of, core_of, z_of, x_of):
        return (y_of * 2 + core_of) * n + z_of * 2 + x_of

    def spread_from_line(block):
        push(block, across_y, side_sems(1))
        push(block, across_x, side_sems(0))
        push(block, sibling, side_sems(2))

    def at_distance(step, act):
        if step == 0:
            act(z, 0)
            return

        @pl.when(z - step >= 0)
        def _():
            act(z - step, 1)

        @pl.when(z + step < lines)
        def _():
            act(z + step, 2)

    def go_on(step, z_of, come_from):
        block = block_at(y, core, z_of, x)
        if come_from != 0:
            arrived(block)
        if come_from != 2:
            @pl.when(z + 1 < lines)
            def _():
                push(block, (dp, me + 2), line_sems(0, step))
        if come_from != 1:
            @pl.when(z >= 1)
            def _():
                push(block, (dp, me - 2), line_sems(1, step))
        spread_from_line(block)

    def line_stage(step):
        at_distance(step, lambda z_of, side: go_on(step, z_of, side))

    def x_stage(step):
        def act(z_of, side):
            block = block_at(y, core, z_of, 1 - x)
            arrived(block)
            push(block, across_y, side_sems(1))
            push(block, sibling, side_sems(2))

        at_distance(step, act)

    def y_stage(step):
        def act(z_of, side):
            for x_of in (x, 1 - x):
                block = block_at(1 - y, core, z_of, x_of)
                arrived(block)
                push(block, sibling, side_sems(2))

        at_distance(step, act)

    def weight_stage(slot):
        if not gather:
            return
        if slot < lines:
            line_stage(slot)
        if 1 <= slot <= lines:
            x_stage(slot - 1)
        if 3 <= slot <= lines + 2:
            y_stage(slot - 3)

    sources = (q_ref, k_ref, v_ref)
    my_rows = pl.ds(pl.multiple_of(me * rows, rows), rows)

    def columns(owner, part):
        return pl.ds(pl.multiple_of(owner * local + part * chunk, chunk), chunk)

    work = [(image, part) for image in range(images) for part in range(chunks)]

    def issue(at):
        if at >= len(work):
            return
        image, part = work[at]
        for which, source in enumerate(sources):
            pltpu.make_async_copy(
                source.at[image, :, columns(me, part)],
                held.at[which, image, part, my_rows, :],
                recv_sem.at[which, image, part],
            ).start()

        @pl.loop(1, n)
        def _(step):
            to = peer(step)
            for which, source in enumerate(sources):
                pltpu.make_async_remote_copy(
                    src_ref=source.at[image, :, columns(to, part)],
                    dst_ref=held.at[which, image, part, my_rows, :],
                    send_sem=send_sem.at[which],
                    recv_sem=recv_sem.at[which, image, part],
                    device_id=(dp, to),
                    device_id_type=MESH,
                ).start()

    halo_copies = [
        pltpu.make_async_remote_copy(
            src_ref=t_ref.at[:, pl.ds(start, HALO), :],
            dst_ref=near.at[:, pl.ds(land, HALO), :],
            send_sem=halo_send.at[side],
            recv_sem=halo_recv.at[side],
            device_id=(dp, to),
            device_id_type=MESH,
        )
        for side, start, land, to in ((0, band - HALO, 0, right), (1, 0, band + HALO, left))
    ]
    for copy in w_copies:
        if gather:
            copy.wait()
    for copy in halo_copies:
        copy.start()
    weight_stage(0)
    issue(0)

    near_copy.wait()
    for copy in halo_copies:
        copy.wait()
    row = lax.broadcasted_iota(jnp.int32, (reach, rows), 0) + (me * band - HALO)
    real = lax.broadcasted_iota(jnp.int32, (reach, near.shape[2]), 0) + (me * band - HALO)
    real = jnp.logical_and(real >= 0, real < n * band)
    for image in range(images):
        index, frac = idx_ref[image], frac_ref[image].astype(jnp.float32)
        fx, fy = frac[0:1, :], frac[1:2, :]
        factors = ((8.0 - fx) * (8.0 - fy), fx * (8.0 - fy), (8.0 - fx) * fy, fx * fy)
        spread = jnp.zeros((reach, rows), jnp.float32)
        for j in range(4):
            spread += jnp.where(index[j : j + 1, :] == row, factors[j], 0.0)
        spread = (spread * (1.0 / 64.0)).astype(jnp.bfloat16)
        wide = jnp.where(real, near[image].astype(jnp.float32), 0.0).astype(jnp.bfloat16)
        target_ref[pl.ds(image * rows, rows), :] = lax.dot_general(
            spread, wide, (((0,), (0,)), ((), ())), preferred_element_type=jnp.float32
        )
    weight_stage(1)
    issue(1)

    block_rows = min(length, 512)
    scale = HD ** (-0.5)
    for at, (image, part) in enumerate(work):
        for which in range(3):
            full = held.at[which, image, part]
            pltpu.make_async_copy(full, full, recv_sem.at[which, image, part]).wait()
        issue(at + 2)
        for head in range(chunk // HD):
            cols = pl.ds(head * HD, HD)
            key = held[1, image, part, :, cols]
            value = held[2, image, part, :, cols]
            for start in range(0, length, block_rows):
                query = held[0, image, part, pl.ds(start, block_rows), cols]
                scores = lax.dot_general(query, key, NT, preferred_element_type=jnp.float32)
                top = jnp.max(scores, axis=-1, keepdims=True)
                prob = jnp.exp((scores - top) * scale)
                mass = jnp.sum(prob, axis=-1, keepdims=True)
                out = jnp.dot(prob.astype(jnp.bfloat16), value, preferred_element_type=jnp.float32)
                mixed[image, part, pl.ds(start, block_rows), cols] = (out / mass).astype(
                    jnp.bfloat16
                )
        pltpu.make_async_copy(
            mixed.at[image, part, my_rows, :], att_ref.at[image, :, columns(me, part)], back_recv
        ).start()

        @pl.loop(1, n)
        def _(step, image=image, part=part):
            to = peer(step)
            pltpu.make_async_remote_copy(
                src_ref=mixed.at[image, part, pl.ds(pl.multiple_of(to * rows, rows), rows), :],
                dst_ref=att_ref.at[image, :, columns(me, part)],
                send_sem=back_send,
                recv_sem=back_recv,
                device_id=(dp, to),
                device_id_type=MESH,
            ).start()

        weight_stage(at + 2)

    if gather:
        for slot in range(len(work) + 2, lines + 3):
            weight_stage(slot)
    pltpu.make_async_copy(att_ref, att_ref, back_recv).wait()

    for copy in small_copies:
        copy.wait()
    if gather:
        @pl.loop(0, n)
        def _(at):
            for y_of in range(2):
                arrived((y_of * 2 + (1 - core)) * n + at)
    else:
        for copy in w_copies:
            copy.wait()

    depth = in_ref.shape[0] // 8

    def attended(c):
        return att_ref[:, :, pl.ds(c * depth, depth)].reshape(total, depth).astype(jnp.float32)

    squares = jnp.zeros((total, 1), jnp.float32)
    for c in range(8):
        wide = attended(c)
        squares += jnp.sum(wide * wide, axis=-1, keepdims=True)
    inv_rms = lax.rsqrt(squares / width + epsilon)

    raw = jnp.zeros((total, in_ref.shape[1]), jnp.float32)
    for c in range(8):
        normed = (attended(c) * inv_rms * gain_ref[:, pl.ds(c * depth, depth)]).astype(jnp.bfloat16)
        raw += jnp.dot(
            normed, in_ref[pl.ds(c * depth, depth), :], preferred_element_type=jnp.float32
        )
    pre_act = raw + bias_in_ref[...]
    gate = 1.0 / (1.0 + jnp.exp(-pre_act))
    hidden = (pre_act * gate).astype(jnp.bfloat16)
    projected = (
        jnp.dot(hidden, out_ref[...], preferred_element_type=jnp.float32) + bias_out_ref[...]
    )
    target = target_ref[...]
    pp = jnp.sum(projected * projected, axis=-1, keepdims=True) + epsilon
    tt = jnp.sum(target * target, axis=-1, keepdims=True) + epsilon
    pt = jnp.sum(projected * target, axis=-1, keepdims=True)
    both = lax.rsqrt(pp) * lax.rsqrt(tt)
    alignment = pt * both
    turned = jnp.transpose(jnp.broadcast_to(alignment, (total, 128)))
    for image in range(images):
        align_ref[image : image + 1, :] = turned[0:1, image * rows : (image + 1) * rows]
    steps = jnp.concatenate(
        [jnp.full((rows, 1), step_ref[image], jnp.int32) for image in range(images)], axis=0
    )
    wave = jnp.cos(0.5 * math.pi * steps.astype(jnp.float32) / TSTEPS)
    factor = -loss_scale * (0.25 + 0.75 * wave * wave)
    d_proj = (factor * both * target - (factor * alignment / pp) * projected).astype(jnp.bfloat16)
    d_hidden = lax.dot_general(d_proj, out_ref[...], NT, preferred_element_type=jnp.float32)
    d_pre = (d_hidden * gate * (1.0 + pre_act * (1.0 - gate))).astype(jnp.bfloat16)
    mean = jnp.sum(d_pre.astype(jnp.float32) * raw, axis=-1, keepdims=True) / (inv_rms * width)
    pull = inv_rms * inv_rms * inv_rms * mean
    for c in range(8):
        cols = pl.ds(c * depth, depth)
        d_normed = lax.dot_general(d_pre, in_ref[cols, :], NT, preferred_element_type=jnp.float32)
        grad = inv_rms * gain_ref[:, cols] * d_normed - attended(c) * pull
        grad_ref[:, :, cols] = grad.astype(jnp.bfloat16).reshape(images, rows, depth)

    for which, source in enumerate(sources):
        sent = source.at[:, :, pl.ds(0, width - local)]
        pltpu.make_async_copy(sent, sent, send_sem.at[which]).wait()
    sent = mixed.at[:, :, pl.ds(0, length - rows), :]
    pltpu.make_async_copy(sent, sent, back_send).wait()
    if gather:
        for kind, count in ((0, lines), (1, n), (2, 2 * n)):
            for j in range(2):
                sent = piece(j, 0, count)
                pltpu.make_async_copy(sent, sent, side_send.at[kind, j]).wait()

        def line_left(side, step, there):
            @pl.when(there)
            def _():
                for j in range(2):
                    sent = piece(j, 0)
                    pltpu.make_async_copy(sent, sent, line_send.at[side, step, j]).wait()

        for step in range(lines):
            line_left(0, step, jnp.logical_and(z - step >= 0, z + 1 < lines))
            line_left(1, step, jnp.logical_and(z + step < lines, z >= 1))


def shards(
    queries,
    keys,
    values,
    teacher,
    resample_index,
    resample_frac,
    timesteps,
    norm_gain,
    proj_in,
    bias_in,
    proj_out,
    bias_out,
):
    n, planes = lax.axis_size("seq"), lax.axis_size("dp")
    images, rows, width = queries.shape
    features = teacher.shape[2]
    hidden = proj_in.shape[1]
    gather = planes == 4 and n % 2 == 0 and proj_in.shape[0] % 16 == 0 and proj_out.shape[0] % 16 == 0
    if not gather:
        proj_in = lax.all_gather(proj_in, ("dp", "seq"), axis=0, tiled=True)
        proj_out = lax.all_gather(proj_out, ("dp", "seq"), axis=0, tiled=True)
    local = width // n
    chunk = min(local, 2 * HD)
    chunks = local // chunk
    length = rows * n
    band = teacher.shape[1]
    vmem = pl.BlockSpec(memory_space=pltpu.VMEM)
    smem = pl.BlockSpec(memory_space=pltpu.SMEM)
    hbm = pl.BlockSpec(memory_space=pltpu.HBM)
    dma = pltpu.SemaphoreType.DMA
    bf16, f32 = jnp.bfloat16, jnp.float32
    return pl.pallas_call(
        functools.partial(align_kernel, n, chunk, gather),
        out_shape=(
            jax.ShapeDtypeStruct((images, rows), f32),
            jax.ShapeDtypeStruct(queries.shape, bf16),
        ),
        in_specs=[hbm, hbm, hbm, hbm, vmem, vmem, smem, hbm, hbm, hbm, hbm, hbm],
        out_specs=(vmem, vmem),
        scratch_shapes=[
            pltpu.VMEM((3, images, chunks, length, chunk), bf16),
            pltpu.VMEM((images, chunks, length, chunk), bf16),
            pltpu.VMEM(queries.shape, bf16),
            pltpu.VMEM((images * rows, features), f32),
            pltpu.VMEM((images, band + 2 * HALO, features), bf16),
            pltpu.VMEM((width, hidden), bf16),
            pltpu.VMEM((hidden, features), bf16),
            pltpu.VMEM((1, width), f32),
            pltpu.VMEM((1, hidden), f32),
            pltpu.VMEM((1, features), f32),
            dma((3,)),
            dma((3, images, chunks)),
            dma,
            dma,
            dma((2,)),
            dma((2,)),
            dma,
            dma((3,)),
            dma((2,)),
            dma((2, planes * n if gather else 1)),
            dma((2, max(n // 2, 1), 2)),
            dma((3, 2)),
        ],
        compiler_params=pltpu.CompilerParams(
            collective_id=0, has_side_effects=True, vmem_limit_bytes=60 * 2**20
        ),
        name="align",
    )(
        queries, keys, values, teacher,
        jnp.transpose(resample_index, (0, 2, 1)), jnp.transpose(resample_frac, (0, 2, 1)),
        timesteps, norm_gain[None], bias_in[None], bias_out[None], proj_in, proj_out,
    )


def solution(mesh):
    return jax.shard_map(
        shards,
        mesh=mesh,
        in_specs=(
            P("dp", "seq", None),
            P("dp", "seq", None),
            P("dp", "seq", None),
            P("dp", "seq", None),
            P("dp", "seq", None),
            P("dp", "seq", None),
            P("dp"),
            P(),
            P(("dp", "seq"), None),
            P(),
            P(("dp", "seq"), None),
            P(),
        ),
        out_specs=(P("dp", "seq"), P("dp", "seq", None)),
        check_vma=False,
    )
```
